128 devices in a mesh: grp: 8 (over x, core), head: 16 (over y, z).
Axes of the slice: x: 4, y: 4, z: 4, core: 2. Of those that a mesh axis runs over, the one named last changes fastest.
Arguments:
- query_in: bfloat16 [64, 2, 8192], P('grp', None, 'head'), may hold values from -6 to 6
- key_in: bfloat16 [64, 2, 8192], P('grp', None, 'head'), may hold values from -6 to 6
- value_in: bfloat16 [64, 2, 8192], P('grp', None, 'head'), may hold values from -6 to 6
- decay_rate: float32 [64], P('head'), may hold values from 0.6 to 0.995
- states: float32 [64, 64, 128, 128], P('grp', 'head'), may hold values from -6 to 6
- attn_gain: float32 [8192], P('head'), may hold values from 0.25 to 1.75
- out_proj: bfloat16 [8192, 6144], P('head', 'grp'), may hold values from -0.0625 to 0.0625
- stream_in: bfloat16 [64, 2, 6144], P('head', None, 'grp'), may hold values from -27 to 27
- ffn_gain: float32 [6144], replicated, may hold values from 0.1 to 1.9
- expert_gate: bfloat16 [16, 4608, 6144], P('head', 'grp'), may hold values from -0.078125 to 0.078125
- expert_up: bfloat16 [16, 4608, 6144], P('head', 'grp'), may hold values from -0.078125 to 0.078125
- expert_down: bfloat16 [16, 4608, 6144], P('head', 'grp'), may hold values from -0.09375 to 0.09375
- routes: int32 [64, 2, 2], P('head'), may hold values from 0 to 15, as said below
- route_weights: float32 [64, 2, 2], P('head'), may hold values from 0.2 to 1
Outputs:
- stream_out: bfloat16 [64, 2, 6144], P('head', None, 'grp')
- states_out: float32 [64, 64, 128, 128], P('grp', 'head')
The draws below stay inside these ranges and needn't reach their ends.
Inputs may be any that keep to these rules, and one draw needn't show every extreme that they name: `routes`: each row names two different experts. Within the 8 token rows of one head index (aligned blocks of 4 requests), no expert is named more than 2 times, and some expert is named exactly 2 times within every such block.
All inputs are finite; a program needn't handle non-finite values.
Results may differ from the reference program's by a relative error of at most 0.0054.
Values may be sent and summed in bfloat16 or wider, within the bound.
No kernel may reach another device: no remote copies, remote signals or barrier semaphores. Data moves between devices by JAX's collectives and lax.ppermute only.
A program may use at most 128 MiB of HBM per device.

```python
import math
import jax
import jax.numpy as jnp
from jax import lax

D = 6144
H = 64
HD = 128
FFW = 4608
POS = 2
CAP = 2
EXPERTS = 16
REQUESTS = 64
BLOCK = 8


def draw_stream_in(key, part):
    key = jax.random.fold_in(key, 5)
    key_base, key_cols, key_rows = jax.random.split(key, 3)
    shape_full = (REQUESTS, POS, D)
    col_scale = jnp.exp(jax.random.uniform(key_cols, (D,), jnp.float32, math.log(0.3), math.log(3.0)))
    base = jnp.clip(jax.random.normal(key_base, shape_full, jnp.float32), -4.0, 4.0)
    row_scale = jnp.exp(jax.random.uniform(key_rows, (REQUESTS, POS, 1), jnp.float32, math.log(0.5), math.log(2.0)))
    return (base * col_scale * row_scale).astype(jnp.bfloat16)


def draw_routes(key, part):
    key = jax.random.fold_in(key, 11)
    key_hot, key_perm, key_lead, key_rows, key_swap = jax.random.split(key, 5)
    blocks = REQUESTS * POS // BLOCK
    hottest = jax.random.randint(key_hot, (), 0, EXPERTS)
    perm_keys = jax.random.split(key_perm, blocks)
    rest = jnp.stack([jax.random.permutation(perm_keys[index], EXPERTS - 1) + 1 for index in range(blocks)])
    offsets = jnp.concatenate([jnp.zeros((blocks, 1), jnp.int32), rest.astype(jnp.int32)], axis=1)
    ordering = (hottest + offsets) % EXPERTS
    leading = jax.random.randint(key_lead, (blocks,), 1, BLOCK)
    shifted = EXPERTS - leading
    positions = jnp.arange(BLOCK, dtype=jnp.int32)
    first_pick = ordering[:, :BLOCK]
    second_pick = jnp.take_along_axis(ordering, (positions[None, :] + shifted[:, None]) % EXPERTS, axis=1)
    paired = jnp.stack([first_pick, second_pick], axis=-1)
    row_keys = jax.random.split(key_rows, blocks)
    shuffled = jnp.stack([jax.random.permutation(row_keys[index], BLOCK) for index in range(blocks)]).astype(jnp.int32)
    paired = jnp.take_along_axis(paired, shuffled[:, :, None], axis=1)
    flips = jax.random.randint(key_swap, (blocks, BLOCK, 1), 0, 2)
    paired = jnp.where(flips == 1, paired[..., ::-1], paired)
    return paired.reshape(REQUESTS, POS, 2).astype(jnp.int32)


def block_scale(rng, extent, pieces, low, top_value):
    def one(axis_at, blocks):
        draws = jax.random.uniform(jax.random.fold_in(jax.random.fold_in(rng, 6), axis_at), (blocks,), jnp.float32, low / len(pieces), top_value / len(pieces))
        return jnp.repeat(jnp.exp(draws), extent[axis_at] // blocks).reshape((-1,) + (1,) * (len(extent) - axis_at - 1))

    gain = one(*pieces[0])
    for cut in pieces[1:]:
        gain = gain * one(*cut)
    return gain


def centred(own_key, shape, width, most, pieces=(), held_as=jnp.bfloat16):
    loudness = block_scale(own_key, shape, pieces, -0.22, 0.18) if pieces else 1.0
    result = jax.random.normal(own_key, shape, jnp.float32) * width * loudness
    return jnp.minimum(jnp.maximum(result, -most), most).astype(held_as)


def setup_inputs(seed: int = 0) -> dict:
    streams_of = jax.random.split(jax.random.key(seed), 15)
    query_in = centred(streams_of[0], (REQUESTS, POS, H * HD), 1.0, 6.0, ((0, 8), (2, 16)))
    key_in = centred(streams_of[1], (REQUESTS, POS, H * HD), 1.0, 6.0, ((0, 8), (2, 16)))
    value_in = centred(streams_of[2], (REQUESTS, POS, H * HD), 1.0, 6.0, ((0, 8), (2, 16)))
    decay_rate = jnp.clip(0.6 + 0.39499998 * jax.random.uniform(streams_of[3], (H,), jnp.float32) ** block_scale(streams_of[3], (H,), ((0, 16),), -0.2, 0.2), 0.6, 0.995)
    states = centred(streams_of[4], (REQUESTS, H, HD, HD), 1.0, 6.0, ((0, 8), (1, 16)), jnp.float32)
    attn_gain = jnp.clip(1.0 + 0.15 * jax.random.normal(streams_of[5], (H * HD,), jnp.float32), 0.25, 1.75)
    out_proj = centred(streams_of[6], (H * HD, D), (H * HD) ** -0.5, 0.0625, ((0, 16), (1, 8)))
    stream_in = draw_stream_in(jax.random.fold_in(streams_of[14], 71), 0)
    ffn_gain = jnp.clip(1.0 + 0.18 * jax.random.normal(streams_of[8], (D,), jnp.float32), 0.1, 1.9)
    expert_gate = centred(streams_of[9], (EXPERTS, FFW, D), D ** -0.5, 0.078125, ((0, 16), (1, 8)))
    expert_up = centred(streams_of[10], (EXPERTS, FFW, D), D ** -0.5, 0.078125, ((0, 16), (1, 8)))
    expert_down = centred(streams_of[11], (EXPERTS, FFW, D), FFW ** -0.5, 0.09375, ((0, 16), (1, 8)))
    routes = draw_routes(jax.random.fold_in(streams_of[14], 71), 0)
    route_weights = jnp.clip(0.2 + 0.8 * jax.random.uniform(streams_of[13], (REQUESTS, POS, 2), jnp.float32) ** block_scale(streams_of[13], (REQUESTS, POS, 2), ((0, 16),), -0.2, 0.2), 0.2, 1.0)
    return {"query_in": query_in, "key_in": key_in, "value_in": value_in, "decay_rate": decay_rate, "states": states, "attn_gain": attn_gain, "out_proj": out_proj, "stream_in": stream_in, "ffn_gain": ffn_gain, "expert_gate": expert_gate, "expert_up": expert_up, "expert_down": expert_down, "routes": routes, "route_weights": route_weights}


EPSILON = 1e-06

def reference(query_in, key_in, value_in, decay_rate, states, attn_gain, out_proj, stream_in, ffn_gain, expert_gate, expert_up, expert_down, routes, route_weights):
    shape_four = (REQUESTS, POS, H, HD)
    queries = query_in.astype(jnp.float32).reshape(shape_four)
    keyset = key_in.reshape(shape_four)
    valueset = value_in.reshape(shape_four)
    memory_state = states
    outputs = []
    for position in range(POS):
        outer = jnp.einsum('rhk,rhv->rhkv', keyset[:, position], valueset[:, position], preferred_element_type=jnp.float32)
        memory_state = decay_rate[None, :, None, None] * memory_state + outer
        outputs.append(jnp.einsum('rhk,rhkv->rhv', queries[:, position], memory_state, precision=lax.Precision.HIGHEST))
    readout = jnp.stack(outputs, axis=1)
    scaled = readout * lax.rsqrt(lax.optimization_barrier(jnp.mean(readout * readout, axis=-1, keepdims=True)) + EPSILON) * attn_gain.reshape(H, HD)
    attended = scaled.astype(jnp.bfloat16).reshape(REQUESTS * POS, H * HD)
    mixed = jnp.dot(attended, out_proj, preferred_element_type=jnp.float32)
    residual = (stream_in.astype(jnp.float32).reshape(REQUESTS * POS, D) + mixed).astype(jnp.bfloat16)
    widened = residual.astype(jnp.float32)
    normed = (widened * lax.rsqrt(lax.optimization_barrier(jnp.mean(widened * widened, axis=-1, keepdims=True)) + EPSILON) * ffn_gain).astype(jnp.bfloat16)
    chosen = routes.reshape(REQUESTS * POS, 2)
    weighting = route_weights.reshape(REQUESTS * POS, 2)
    most_rows = min(CAP * (REQUESTS * POS // BLOCK), REQUESTS * POS)
    contract = (((1,), (1,)), ((), ()))

    def one_expert(carry, expert):
        named = lax.optimization_barrier(jnp.sum(jnp.where(chosen == expert, weighting, jnp.zeros_like(weighting)), axis=1))
        hits = jnp.any(chosen == expert, axis=1)
        order = jnp.argsort(jnp.where(hits, 0, 1).astype(jnp.int32), stable=True)[:most_rows].astype(jnp.int32)
        taken = normed[order]
        gate_out = lax.dot_general(taken, expert_gate[expert], contract, preferred_element_type=jnp.float32)
        up_out = lax.dot_general(taken, expert_up[expert], contract, preferred_element_type=jnp.float32)
        activated = (jax.nn.silu(gate_out) * up_out).astype(jnp.bfloat16)
        produced = jnp.dot(activated, expert_down[expert], preferred_element_type=jnp.float32)
        carry = carry.at[order].add(named[order][:, None] * produced)
        return (carry, None)
    moe, unused = lax.scan(one_expert, jnp.zeros((REQUESTS * POS, D), jnp.float32), jnp.arange(EXPERTS, dtype=jnp.int32))
    stream_out = (residual.astype(jnp.float32) + moe).astype(jnp.bfloat16).reshape(REQUESTS, POS, D)
    return (stream_out, memory_state)
```

```python
import jax
import jax.numpy as jnp
from jax import lax
from jax.sharding import PartitionSpec as P

CAP = 2


EPSILON = 1e-06


def expert_rows(flattened, gate_local, up_local, down_local):
    contract = (((1,), (1,)), ((), ()))
    gate_out = lax.dot_general(flattened, gate_local, contract, preferred_element_type=jnp.float32)
    upward = lax.dot_general(flattened, up_local, contract, preferred_element_type=jnp.float32)
    activated = (jax.nn.silu(gate_out) * upward).astype(jnp.bfloat16)
    return jnp.dot(activated, down_local, preferred_element_type=jnp.float32)


def body(
    query_in,
    key_in,
    value_in,
    decay_rate,
    states,
    attn_gain,
    out_proj,
    stream_in,
    ffn_gain,
    expert_gate,
    expert_up,
    expert_down,
    routes,
    route_weights,
):
    requests_here, positions, width_here = query_in.shape
    head_count = states.shape[1]
    head_size = states.shape[2]
    shape_four = (requests_here, positions, head_count, head_size)
    queries = query_in.astype(jnp.float32).reshape(shape_four)
    keyset = key_in.reshape(shape_four)
    valueset = value_in.reshape(shape_four)
    memory_state = states
    outputs = []
    for position in range(positions):
        outer = jnp.einsum(
            "rhk,rhv->rhkv",
            keyset[:, position],
            valueset[:, position],
            preferred_element_type=jnp.float32,
        )
        memory_state = decay_rate[None, :, None, None] * memory_state + outer
        outputs.append(
            jnp.einsum(
                "rhk,rhkv->rhv", queries[:, position], memory_state, precision=lax.Precision.HIGHEST
            )
        )
    readout = jnp.stack(outputs, axis=1)
    scaled = (
        readout
        * lax.rsqrt(jnp.mean(readout * readout, axis=-1, keepdims=True) + EPSILON)
        * attn_gain.reshape(head_count, head_size)
    )
    attended = scaled.astype(jnp.bfloat16).reshape(requests_here * positions, width_here)
    groups = lax.axis_size("grp")
    heads = lax.axis_size("head")
    rows_here = requests_here * positions
    everyone = lax.all_to_all(
        jnp.broadcast_to(attended[None], (groups, rows_here, width_here)),
        "grp",
        split_axis=0,
        concat_axis=0,
        tiled=True,
    ).reshape(groups * rows_here, width_here)
    partial_sums = jnp.dot(everyone, out_proj, preferred_element_type=jnp.float32)
    shares = lax.all_to_all(
        partial_sums.astype(jnp.bfloat16).reshape(heads, -1, partial_sums.shape[1]),
        "head",
        split_axis=0,
        concat_axis=0,
        tiled=True,
    )
    mixed = jnp.sum(shares.astype(jnp.float32), axis=0)
    tokens_here = mixed.shape[0]
    columns = mixed.shape[1]
    model_width = columns * lax.axis_size("grp")
    residual = (stream_in.astype(jnp.float32).reshape(tokens_here, columns) + mixed).astype(
        jnp.bfloat16
    )
    experts = lax.axis_size("head") * expert_gate.shape[0]
    chosen = routes.reshape(tokens_here, 2)
    weighting = route_weights.reshape(tokens_here, 2)
    onehot = (
        (chosen[:, :, None] == jnp.arange(experts, dtype=jnp.int32)[None, None, :])
        .astype(jnp.int32)
        .reshape(tokens_here * 2, experts)
    )
    earlier = jnp.cumsum(onehot, axis=0) - onehot
    slot_index = jnp.sum(earlier * onehot, axis=1).reshape(tokens_here, 2)
    slot_code = chosen * CAP + slot_index
    slots_all = experts * CAP
    selection = (
        jnp.arange(slots_all, dtype=jnp.int32)[:, None, None] == slot_code[None, :, :]
    ).astype(jnp.float32)
    picker = jnp.sum(selection, axis=2).astype(jnp.bfloat16)
    combiner = jnp.transpose(jnp.sum(selection * weighting[None, :, :], axis=2))
    gate_local = expert_gate[0]
    up_local = expert_up[0]
    down_local = expert_down[0]
    slot_rows = (
        jnp.dot(picker, residual, preferred_element_type=jnp.float32)
        .astype(jnp.bfloat16)
        .reshape(1, experts, CAP, columns)
    )
    arrived = lax.all_to_all(
        jnp.broadcast_to(slot_rows, (groups, experts, CAP, columns)).reshape(-1, CAP, columns),
        ("grp", "head"),
        split_axis=0,
        concat_axis=0,
        tiled=True,
    )
    full_rows = (
        arrived.reshape(groups, heads * CAP, columns)
        .transpose(1, 0, 2)
        .reshape(heads * CAP, model_width)
        .astype(jnp.float32)
    )
    normed = (
        full_rows
        * lax.rsqrt(jnp.mean(full_rows * full_rows, axis=-1, keepdims=True) + EPSILON)
        * ffn_gain
    ).astype(jnp.bfloat16)
    produced = expert_rows(normed, gate_local, up_local, down_local)
    outgoing = (
        produced.astype(jnp.bfloat16)
        .reshape(heads * CAP, groups, columns)
        .transpose(1, 0, 2)
        .reshape(-1, CAP, columns)
    )
    returned = lax.all_to_all(
        outgoing, ("grp", "head"), split_axis=0, concat_axis=0, tiled=True
    ).reshape(groups, slots_all, columns)
    moe = jnp.dot(
        combiner,
        jnp.sum(returned.astype(jnp.float32), axis=0),
        precision=lax.Precision.HIGHEST,
        preferred_element_type=jnp.float32,
    )
    stream_out = (residual.astype(jnp.float32) + moe).astype(jnp.bfloat16).reshape(stream_in.shape)
    return (stream_out, memory_state)


def solution(mesh):
    return jax.shard_map(
        body,
        mesh=mesh,
        in_specs=(
            P("grp", None, "head"),
            P("grp", None, "head"),
            P("grp", None, "head"),
            P("head"),
            P("grp", "head", None, None),
            P("head"),
            P("head", "grp"),
            P("head", None, "grp"),
            P(),
            P("head", "grp", None),
            P("head", "grp", None),
            P("head", "grp", None),
            P("head", None, None),
            P("head", None, None),
        ),
        out_specs=(P("head", None, "grp"), P("grp", "head", None, None)),
        check_vma=False,
    )
```

```python
import jax
import jax.numpy as jnp
from jax import lax
from jax.experimental import pallas as pl
from jax.experimental.pallas import tpu as pltpu
from jax.sharding import PartitionSpec as P

CAP = 2
HIDDEN_STEPS = 4
DOWN_STEPS = 4
AHEAD = 4


EPSILON = 1e-06


def in_hbm(array):
    return pltpu.with_memory_space_constraint(array, pltpu.HBM)


ROWS_CONTRACT = (((1,), (1,)), ((), ()))


def readout_kernel(
    query_in, key_in, value_in, decay_in, gain_in, states_ref, out_ref,
    query_ref, key_ref, value_ref, decay_ref, gain_ref, held, read, rows, small_sems, sems,
):
    requests, positions, _ = query_ref.shape
    heads, size = states_ref.shape[1], states_ref.shape[2]
    small = [
        pltpu.make_async_copy(source, target, small_sems.at[index])
        for index, (source, target) in enumerate(
            (
                (query_in, query_ref),
                (key_in, key_ref),
                (value_in, value_ref),
                (decay_in, decay_ref),
                (gain_in, gain_ref),
            )
        )
    ]
    small[0].start()
    copies = [
        pltpu.make_async_copy(states_ref.at[request], held.at[request], sems.at[request])
        for request in range(requests)
    ]
    for copy in copies:
        copy.start()
    for copy in small[1:]:
        copy.start()
    small[0].wait()
    for request in range(requests):
        copies[request].wait()
        for head in range(heads):
            columns = slice(head * size, (head + 1) * size)
            state = held[request, head]
            high = state.astype(jnp.bfloat16)
            low = (state - high.astype(jnp.float32)).astype(jnp.bfloat16)
            query = query_ref[request, :, columns]
            read[request, :, columns] = jnp.dot(
                jnp.concatenate([query, query], axis=1),
                jnp.concatenate([high, low], axis=0),
                preferred_element_type=jnp.float32,
            )
    for copy in small[1:]:
        copy.wait()
    first = lax.broadcasted_iota(jnp.int32, (requests, positions, size), 1) == 0
    for head in range(heads):
        columns = slice(head * size, (head + 1) * size)
        decay = decay_ref[head]
        query = query_ref[:, :, columns].astype(jnp.float32)
        keys = key_ref[:, :, columns].astype(jnp.float32)
        values = value_ref[:, :, columns].astype(jnp.float32)
        with_first = jnp.sum(query * keys[:, 0:1, :], axis=2, keepdims=True) * values[:, 0:1, :]
        with_own = jnp.sum(query * keys, axis=2, keepdims=True) * values
        once = decay * read[:, :, columns] + with_first
        readout = jnp.where(first, once, decay * once + with_own)
        scaled = (
            readout
            * lax.rsqrt(jnp.mean(readout * readout, axis=2, keepdims=True) + EPSILON)
            * gain_ref[0:1, columns][None]
        )
        for request in range(requests):
            rows[request * positions : (request + 1) * positions, columns] = scaled[request]
    attended = rows[...].astype(jnp.bfloat16)
    for copy in range(out_ref.shape[0]):
        out_ref[copy] = attended


def readouts(query_in, key_in, value_in, decay_rate, attn_gain, states, copies):
    requests, positions, width = query_in.shape
    vmem = pl.BlockSpec(memory_space=pltpu.VMEM)
    return pl.pallas_call(
        readout_kernel,
        out_shape=jax.ShapeDtypeStruct((copies, requests * positions, width), jnp.bfloat16),
        in_specs=[pl.BlockSpec(memory_space=pltpu.HBM)] * 6,
        out_specs=vmem,
        scratch_shapes=[
            pltpu.VMEM(query_in.shape, jnp.bfloat16),
            pltpu.VMEM(query_in.shape, jnp.bfloat16),
            pltpu.VMEM(query_in.shape, jnp.bfloat16),
            pltpu.SMEM(decay_rate.shape, jnp.float32),
            pltpu.VMEM((1, width), jnp.float32),
            pltpu.VMEM(states.shape, jnp.float32),
            pltpu.VMEM(query_in.shape, jnp.float32),
            pltpu.VMEM((requests * positions, width), jnp.float32),
            pltpu.SemaphoreType.DMA((5,)),
            pltpu.SemaphoreType.DMA((requests,)),
        ],
        compiler_params=pltpu.CompilerParams(vmem_limit_bytes=32 * 2**20),
        cost_estimate=pl.CostEstimate(flops=10**7, bytes_accessed=states.size * 4, transcendentals=0),
        name="readouts",
    )(*(in_hbm(array) for array in (query_in, key_in, value_in, decay_rate, attn_gain.reshape(1, width), states)))


def experts_kernel(
    rows_ref, gain_ref, gate_in, up_in, down_in, out_ref, normed, gate_ref, up_ref, down_ref, activated, sems
):
    hidden, width = gate_in.shape
    columns = rows_ref.shape[2]
    shards = width // columns
    rows = rows_ref.shape[0] * rows_ref.shape[1] // shards
    blocks = rows_ref.shape[0] // shards
    tile = hidden // HIDDEN_STEPS
    wide = shards // DOWN_STEPS
    steps = HIDDEN_STEPS + DOWN_STEPS

    def copies(step):
        if step < HIDDEN_STEPS:
            cut = pl.ds(step * tile, tile)
            parts = ((gate_in.at[cut], gate_ref.at[cut]), (up_in.at[cut], up_ref.at[cut]))
        else:
            cut = pl.ds((step - HIDDEN_STEPS) * wide * columns, wide * columns)
            halves = (pl.ds(0, hidden // 2), pl.ds(hidden // 2, hidden // 2))
            parts = [(down_in.at[half, cut], down_ref.at[half, cut]) for half in halves]
        return [
            pltpu.make_async_copy(source, target, sems.at[step, index])
            for index, (source, target) in enumerate(parts)
        ]

    def begin(step):
        if step < steps:
            for copy in copies(step):
                copy.start()

    def finish(step):
        for copy in copies(step):
            copy.wait()
        begin(step + AHEAD)

    for step in range(AHEAD):
        begin(step)
    squares = jnp.zeros((rows, 1), jnp.float32)
    for shard in range(shards):
        arrived = rows_ref[shard * blocks : (shard + 1) * blocks].reshape(rows, columns)
        normed[:, shard * columns : (shard + 1) * columns] = arrived
        arrived = arrived.astype(jnp.float32)
        squares = squares + jnp.sum(arrived * arrived, axis=1, keepdims=True)
    scale = lax.rsqrt(squares / width + EPSILON)
    for shard in range(shards):
        cut = slice(shard * columns, (shard + 1) * columns)
        normed[:, cut] = (normed[:, cut].astype(jnp.float32) * scale * gain_ref[:, cut]).astype(jnp.bfloat16)
    for step in range(HIDDEN_STEPS):
        finish(step)
        cut = slice(step * tile, (step + 1) * tile)
        gate = lax.dot_general(gate_ref[cut], normed[...], ROWS_CONTRACT, preferred_element_type=jnp.float32)
        upward = lax.dot_general(up_ref[cut], normed[...], ROWS_CONTRACT, preferred_element_type=jnp.float32)
        activated[cut, :] = (gate / (1.0 + jnp.exp(-gate)) * upward).astype(jnp.bfloat16)
    for step in range(DOWN_STEPS):
        finish(HIDDEN_STEPS + step)
        for shard in range(step * wide, (step + 1) * wide):
            produced = lax.dot_general(
                activated[...],
                down_ref[:, shard * columns : (shard + 1) * columns],
                (((0,), (0,)), ((), ())),
                preferred_element_type=jnp.float32,
            )
            out_ref[shard * blocks : (shard + 1) * blocks] = produced.astype(jnp.bfloat16).reshape(
                blocks, rows // blocks, columns
            )


def expert_rows(arrived, gain, gate, up, down):
    hidden, width = gate.shape
    rows = arrived.shape[0] * arrived.shape[1] * arrived.shape[2] // width
    vmem = pl.BlockSpec(memory_space=pltpu.VMEM)
    hbm = pl.BlockSpec(memory_space=pl.ANY)
    return pl.pallas_call(
        experts_kernel,
        out_shape=jax.ShapeDtypeStruct(arrived.shape, jnp.bfloat16),
        in_specs=[vmem, vmem, hbm, hbm, hbm],
        out_specs=vmem,
        scratch_shapes=[
            pltpu.VMEM((rows, width), jnp.bfloat16),
            pltpu.VMEM((hidden, width), jnp.bfloat16),
            pltpu.VMEM((hidden, width), jnp.bfloat16),
            pltpu.VMEM((hidden, width), jnp.bfloat16),
            pltpu.VMEM((hidden, rows), jnp.bfloat16),
            pltpu.SemaphoreType.DMA((HIDDEN_STEPS + DOWN_STEPS, 2)),
        ],
        compiler_params=pltpu.CompilerParams(vmem_limit_bytes=48 * 2**20),
        cost_estimate=pl.CostEstimate(flops=6 * rows * hidden * width, bytes_accessed=6 * hidden * width, transcendentals=0),
        name="experts",
    )(arrived, gain.reshape(1, width), in_hbm(gate), in_hbm(up), in_hbm(down))


def body(
    query_in,
    key_in,
    value_in,
    decay_rate,
    states,
    attn_gain,
    out_proj,
    stream_in,
    ffn_gain,
    expert_gate,
    expert_up,
    expert_down,
    routes,
    route_weights,
):
    requests_here, positions, width_here = query_in.shape
    head_count = states.shape[1]
    head_size = states.shape[2]
    shape_four = (requests_here, positions, head_count, head_size)
    groups = lax.axis_size("grp")
    heads = lax.axis_size("head")
    rows_here = requests_here * positions
    attended = readouts(query_in, key_in, value_in, decay_rate, attn_gain, states, groups)
    attended, keys, values, decay, chosen, weighting, stream = lax.optimization_barrier(
        (attended, key_in, value_in, decay_rate, routes, route_weights, stream_in)
    )
    everyone = lax.all_to_all(attended, "grp", split_axis=0, concat_axis=0, tiled=True)
    keyset = keys.astype(jnp.float32).reshape(shape_four)
    valueset = values.astype(jnp.float32).reshape(shape_four)
    memory_state = states
    for position in range(positions):
        memory_state = (
            decay[None, :, None, None] * memory_state
            + keyset[:, position, :, :, None] * valueset[:, position, :, None, :]
        )
    tokens_here = stream_in.shape[0] * positions
    columns = stream_in.shape[2]
    stream = stream.astype(jnp.float32).reshape(tokens_here, columns)
    experts = lax.axis_size("head") * expert_gate.shape[0]
    chosen = chosen.reshape(tokens_here, 2)
    weighting = weighting.reshape(tokens_here, 2)
    onehot = (
        (chosen[:, :, None] == jnp.arange(experts, dtype=jnp.int32)[None, None, :])
        .astype(jnp.int32)
        .reshape(tokens_here * 2, experts)
    )
    earlier = jnp.cumsum(onehot, axis=0) - onehot
    slot_index = jnp.sum(earlier * onehot, axis=1).reshape(tokens_here, 2)
    slot_code = chosen * CAP + slot_index
    slots_all = experts * CAP
    selection = (
        jnp.arange(slots_all, dtype=jnp.int32)[:, None, None] == slot_code[None, :, :]
    ).astype(jnp.float32)
    picker = jnp.sum(selection, axis=2).astype(jnp.bfloat16)
    combiner = jnp.transpose(jnp.sum(selection * weighting[None, :, :], axis=2))
    everyone, memory_state, stream, picker, combiner = lax.optimization_barrier(
        (everyone, memory_state, stream, picker, combiner)
    )
    partial_sums = jnp.dot(
        everyone.reshape(groups * rows_here, width_here), out_proj, preferred_element_type=jnp.float32
    )
    shares = lax.all_to_all(
        partial_sums.astype(jnp.bfloat16).reshape(heads, -1, partial_sums.shape[1]),
        "head",
        split_axis=0,
        concat_axis=0,
        tiled=True,
    )
    mixed = jnp.sum(shares.astype(jnp.float32), axis=0)
    residual = (stream + mixed).astype(jnp.bfloat16)
    slot_rows = (
        jnp.dot(picker, residual, preferred_element_type=jnp.float32)
        .astype(jnp.bfloat16)
        .reshape(1, experts, CAP, columns)
    )
    arrived = lax.all_to_all(
        jnp.broadcast_to(slot_rows, (groups, experts, CAP, columns)).reshape(-1, CAP, columns),
        ("grp", "head"),
        split_axis=0,
        concat_axis=0,
        tiled=True,
    )
    outgoing = expert_rows(arrived, ffn_gain, expert_gate[0], expert_up[0], expert_down[0])
    returned = lax.all_to_all(
        outgoing, ("grp", "head"), split_axis=0, concat_axis=0, tiled=True
    ).reshape(groups, slots_all, columns)
    moe = jnp.dot(
        combiner,
        jnp.sum(returned.astype(jnp.float32), axis=0),
        precision=lax.Precision.HIGHEST,
        preferred_element_type=jnp.float32,
    )
    stream_out = (residual.astype(jnp.float32) + moe).astype(jnp.bfloat16).reshape(stream_in.shape)
    return (stream_out, memory_state)


def solution(mesh):
    return jax.shard_map(
        body,
        mesh=mesh,
        in_specs=(
            P("grp", None, "head"),
            P("grp", None, "head"),
            P("grp", None, "head"),
            P("head"),
            P("grp", "head", None, None),
            P("head"),
            P("head", "grp"),
            P("head", None, "grp"),
            P(),
            P("head", "grp", None),
            P("head", "grp", None),
            P("head", "grp", None),
            P("head", None, None),
            P("head", None, None),
        ),
        out_specs=(P("head", None, "grp"), P("grp", "head", None, None)),
        check_vma=False,
    )
```

```python
import jax
import jax.numpy as jnp
from jax import lax
from jax.experimental import pallas as pl
from jax.experimental.pallas import tpu as pltpu
from jax.sharding import PartitionSpec as P

CAP = 2
PLACES = (0, 1, 3, 2)
FIRST_HEAD = 11
FIRST_PLACE = 3
HIDDEN_STEPS = 4
DOWN_STEPS = 4
AHEAD = 4


EPSILON = 1e-06


def in_hbm(array):
    return pltpu.with_memory_space_constraint(array, pltpu.HBM)


def heads_in_order(count):
    return [FIRST_HEAD] + [head for head in range(count) if head != FIRST_HEAD]


def places_in_order(count):
    return [FIRST_PLACE] + [place for place in range(count) if place != FIRST_PLACE]


ROWS_CONTRACT = (((1,), (1,)), ((), ()))


def attend_kernel(
    query_in, key_in, value_in, decay_in, gain_in, routes_in, weights_in, stream_in, ffn_gain_in, states_in,
    out_ref, picker_ref, combiner_ref, stream_out, ffn_gain_out, held, left, right, faded_twice,
    query_ref, key_ref, value_ref, decay_ref, gain_ref, routes_ref, weights_ref, stream_ref, read, rows, small_sems, in_sems,
):
    requests, positions, _ = query_ref.shape
    heads, size = held.shape[1], held.shape[2]
    pairs = (
        (query_in, query_ref),
        (key_in, key_ref),
        (value_in, value_ref),
        (decay_in, decay_ref),
        (gain_in, gain_ref),
        (routes_in, routes_ref),
        (weights_in, weights_ref),
        (stream_in, stream_ref),
        (ffn_gain_in, ffn_gain_out),
    )
    small = [
        pltpu.make_async_copy(source, target, small_sems.at[index]) for index, (source, target) in enumerate(pairs)
    ]
    arriving = [
        pltpu.make_async_copy(states_in.at[request], held.at[request], in_sems.at[request])
        for request in range(requests)
    ]
    arriving[0].start()
    for copy in small[:4]:
        copy.start()
    for copy in arriving[1:]:
        copy.start()
    for copy in small[4:]:
        copy.start()
    for copy in small[:4]:
        copy.wait()

    first_part, own_part = [], []
    for head in range(heads):
        columns = slice(head * size, (head + 1) * size)
        query = query_ref[:, :, columns].astype(jnp.float32)
        keys = key_ref[:, :, columns].astype(jnp.float32)
        values = value_ref[:, :, columns].astype(jnp.float32)
        first_key, first_value = keys[:, 0:1, :], values[:, 0:1, :]
        first_part.append(jnp.sum(query * first_key, axis=2, keepdims=True) * first_value)
        own_part.append(jnp.sum(query * keys, axis=2, keepdims=True) * values)
        faded = decay_ref[head] * first_value
        faded_twice[:, columns] = jnp.full((1, size), decay_ref[head] * decay_ref[head], jnp.float32)
        high = faded.astype(jnp.bfloat16).astype(jnp.float32)
        middle = (faded - high).astype(jnp.bfloat16).astype(jnp.float32)
        left[:, :, columns] = jnp.concatenate([first_key, first_key, first_key, keys[:, 1:2, :]], axis=1)
        right[:, :, columns] = jnp.concatenate([high, middle, faded - high - middle, values[:, 1:2, :]], axis=1)

    for request in range(requests):
        arriving[request].wait()
        for head in range(heads):
            columns = slice(head * size, (head + 1) * size)
            state = held[request, head]
            high = state.astype(jnp.bfloat16)
            low = (state - high.astype(jnp.float32)).astype(jnp.bfloat16)
            query = query_ref[request, :, columns]
            read[request, :, columns] = jnp.dot(
                jnp.concatenate([query, query], axis=1),
                jnp.concatenate([high, low], axis=0),
                preferred_element_type=jnp.float32,
            )

    for copy in small[4:]:
        copy.wait()
    first = lax.broadcasted_iota(jnp.int32, (requests, positions, size), 1) == 0
    for head in range(heads):
        columns = slice(head * size, (head + 1) * size)
        decay = decay_ref[head]
        once = decay * read[:, :, columns] + first_part[head]
        readout = jnp.where(first, once, decay * once + own_part[head])
        scaled = (
            readout
            * lax.rsqrt(jnp.mean(readout * readout, axis=2, keepdims=True) + EPSILON)
            * gain_ref[0:1, columns][None]
        )
        for request in range(requests):
            rows[request * positions : (request + 1) * positions, columns] = scaled[request]
    out_ref[...] = rows[...].astype(jnp.bfloat16)

    token_count, choices = picker_ref.shape[1], routes_ref.shape[1]
    chosen, weights = [], []
    for token in range(token_count):
        for choice in range(choices):
            place = (token % positions, choice, token // positions)
            chosen.append(routes_ref[place])
            weights.append(weights_ref[place])
    slot_down = lax.broadcasted_iota(jnp.int32, picker_ref.shape, 0)
    token_across = lax.broadcasted_iota(jnp.int32, picker_ref.shape, 1)
    token_down = lax.broadcasted_iota(jnp.int32, combiner_ref.shape, 0)
    slot_across = lax.broadcasted_iota(jnp.int32, combiner_ref.shape, 1)
    picker = jnp.zeros(picker_ref.shape, jnp.float32)
    combiner = jnp.zeros(combiner_ref.shape, jnp.float32)
    for index, expert in enumerate(chosen):
        position = jnp.where(expert == FIRST_HEAD, 0, expert + (expert < FIRST_HEAD).astype(jnp.int32))
        slot = position * CAP
        for earlier in chosen[:index]:
            slot = slot + (earlier == expert).astype(jnp.int32)
        token = index // choices
        picker = jnp.where((slot_down == slot) & (token_across == token), 1.0, picker)
        combiner = jnp.where((slot_across == slot) & (token_down == token), weights[index], combiner)
    picker_ref[...] = picker.astype(jnp.bfloat16)
    combiner_ref[...] = combiner
    stream_out[...] = stream_ref[...].astype(jnp.float32).reshape(stream_out.shape)


def attend(
    query_in, key_in, value_in, decay_rate, attn_gain, routes, route_weights, stream_in, ffn_gain, states, slots
):
    requests, positions, width = query_in.shape
    tokens = stream_in.shape[0] * stream_in.shape[1]
    routes, route_weights = (jnp.transpose(array, (1, 2, 0)) for array in (routes, route_weights))
    vmem = pl.BlockSpec(memory_space=pltpu.VMEM)
    anywhere = pl.BlockSpec(memory_space=pl.ANY)
    inputs = (
        query_in, key_in, value_in, decay_rate, attn_gain.reshape(1, width), routes, route_weights, stream_in,
        ffn_gain.reshape(1, -1), states,
    )
    return pl.pallas_call(
        attend_kernel,
        out_shape=[
            pltpu.VMEM((requests * positions, width), jnp.bfloat16),
            pltpu.VMEM((slots, tokens), jnp.bfloat16),
            pltpu.VMEM((tokens, slots), jnp.float32),
            pltpu.VMEM((tokens, stream_in.shape[2]), jnp.float32),
            pltpu.VMEM((1, ffn_gain.shape[0]), jnp.float32),
            pltpu.VMEM(states.shape, jnp.float32),
            pltpu.VMEM((requests, 4, width), jnp.float32),
            pltpu.VMEM((requests, 4, width), jnp.float32),
            pltpu.VMEM((1, width), jnp.float32),
        ],
        in_specs=[anywhere] * len(inputs),
        out_specs=[vmem] * 9,
        scratch_shapes=[
            pltpu.VMEM(query_in.shape, jnp.bfloat16),
            pltpu.VMEM(query_in.shape, jnp.bfloat16),
            pltpu.VMEM(query_in.shape, jnp.bfloat16),
            pltpu.SMEM(decay_rate.shape, jnp.float32),
            pltpu.VMEM((1, width), jnp.float32),
            pltpu.SMEM(routes.shape, jnp.int32),
            pltpu.SMEM(route_weights.shape, jnp.float32),
            pltpu.VMEM(stream_in.shape, jnp.bfloat16),
            pltpu.VMEM(query_in.shape, jnp.float32),
            pltpu.VMEM((requests * positions, width), jnp.float32),
            pltpu.SemaphoreType.DMA((9,)),
            pltpu.SemaphoreType.DMA((requests,)),
        ],
        compiler_params=pltpu.CompilerParams(vmem_limit_bytes=32 * 2**20),
        cost_estimate=pl.CostEstimate(flops=10**7, bytes_accessed=states.size * 4, transcendentals=0),
        name="attend",
    )(*(in_hbm(array) for array in inputs))


def project_kernel(place_ref, own_ref, second_ref, third_ref, fourth_ref, weights_ref, out_ref, everyone):
    place = place_ref[0]
    rows = own_ref.shape[0]
    blocks, each, _ = out_ref.shape
    for index, ref in zip(PLACES, (own_ref, second_ref, third_ref, fourth_ref)):
        everyone[pl.ds(pl.multiple_of((place ^ index) * rows, rows), rows), :] = ref[...]
    partial = jnp.dot(everyone[...], weights_ref[...], preferred_element_type=jnp.float32).astype(jnp.bfloat16)
    for position, block in enumerate(heads_in_order(blocks)):
        out_ref[position] = partial[block * each : (block + 1) * each]


def project(place, gathered, weights, blocks):
    rows = len(gathered) * gathered[0].shape[0]
    vmem = pl.BlockSpec(memory_space=pltpu.VMEM)
    return pl.pallas_call(
        project_kernel,
        out_shape=jax.ShapeDtypeStruct((blocks, rows // blocks, weights.shape[1]), jnp.bfloat16),
        in_specs=[pl.BlockSpec(memory_space=pltpu.SMEM)] + [vmem] * 5,
        out_specs=vmem,
        scratch_shapes=[pltpu.VMEM((rows, weights.shape[0]), jnp.bfloat16)],
        compiler_params=pltpu.CompilerParams(vmem_limit_bytes=8 * 2**20),
        cost_estimate=pl.CostEstimate(flops=2 * rows * weights.size, bytes_accessed=2 * weights.size, transcendentals=0),
        name="project",
    )(place, *gathered, weights)


def update_kernel(states_ref, left_ref, right_ref, faded_ref, states_out, updated, sems):
    requests, heads, size, _ = states_ref.shape
    leaving = []
    for request in range(requests):
        for head in range(heads):
            columns = slice(head * size, (head + 1) * size)
            added = lax.dot_general(
                left_ref[request, :, columns].astype(jnp.bfloat16),
                right_ref[request, :, columns].astype(jnp.bfloat16),
                (((0,), (0,)), ((), ())),
                preferred_element_type=jnp.float32,
            )
            updated[request, head] = faded_ref[:, columns] * states_ref[request, head] + added
        leaving.append(pltpu.make_async_copy(updated.at[request], states_out.at[request], sems.at[request]))
        leaving[-1].start()
    for copy in leaving:
        copy.wait()


def update(states, left, right, faded_twice):
    vmem = pl.BlockSpec(memory_space=pltpu.VMEM)
    return pl.pallas_call(
        update_kernel,
        out_shape=pltpu.HBM(states.shape, jnp.float32),
        in_specs=[vmem] * 4,
        out_specs=pl.BlockSpec(memory_space=pl.ANY),
        scratch_shapes=[pltpu.VMEM(states.shape, jnp.float32), pltpu.SemaphoreType.DMA((states.shape[0],))],
        compiler_params=pltpu.CompilerParams(vmem_limit_bytes=16 * 2**20),
        cost_estimate=pl.CostEstimate(flops=10**7, bytes_accessed=states.size * 4, transcendentals=0),
        name="update",
    )(states, left, right, faded_twice)


def experts_kernel(
    core_ref, own_ref, partner_ref, gain_ref, gate_in, up_in, down_in, out_ref,
    normed, gate_ref, up_ref, down_ref, activated, sems,
):
    hidden, width = gate_in.shape
    columns = own_ref.shape[2]
    shards = width // columns
    places = places_in_order(shards // 2)
    blocks = own_ref.shape[0] // len(places)
    rows = blocks * own_ref.shape[1]
    tile = hidden // HIDDEN_STEPS
    wide = shards // DOWN_STEPS
    steps = HIDDEN_STEPS + DOWN_STEPS

    def copies(step):
        if step < HIDDEN_STEPS:
            cut = pl.ds(step * tile, tile)
            parts = ((gate_in.at[cut], gate_ref.at[cut]), (up_in.at[cut], up_ref.at[cut]))
        else:
            cut = pl.ds((step - HIDDEN_STEPS) * wide * columns, wide * columns)
            halves = (pl.ds(0, hidden // 2), pl.ds(hidden // 2, hidden // 2))
            parts = [(down_in.at[half, cut], down_ref.at[half, cut]) for half in halves]
        return [
            pltpu.make_async_copy(source, target, sems.at[step, index])
            for index, (source, target) in enumerate(parts)
        ]

    def begin(step):
        if step < steps:
            for copy in copies(step):
                copy.start()

    def finish(step):
        for copy in copies(step):
            copy.wait()
        begin(step + AHEAD)

    for step in range(AHEAD):
        begin(step)
    core = core_ref[0]
    squares = jnp.zeros((rows, 1), jnp.float32)
    for ref, side in ((own_ref, core), (partner_ref, 1 - core)):
        for index, place in enumerate(places):
            arrived = ref[index * blocks : (index + 1) * blocks].reshape(rows, columns)
            normed[:, pl.ds(pl.multiple_of((2 * place + side) * columns, 128), columns)] = arrived
            arrived = arrived.astype(jnp.float32)
            squares = squares + jnp.sum(arrived * arrived, axis=1, keepdims=True)
    scale = lax.rsqrt(squares / width + EPSILON)
    for shard in range(shards):
        cut = slice(shard * columns, (shard + 1) * columns)
        normed[:, cut] = (normed[:, cut].astype(jnp.float32) * scale * gain_ref[:, cut]).astype(jnp.bfloat16)
    for step in range(HIDDEN_STEPS):
        finish(step)
        cut = slice(step * tile, (step + 1) * tile)
        gate = lax.dot_general(gate_ref[cut], normed[...], ROWS_CONTRACT, preferred_element_type=jnp.float32)
        upward = lax.dot_general(up_ref[cut], normed[...], ROWS_CONTRACT, preferred_element_type=jnp.float32)
        activated[cut, :] = (gate / (1.0 + jnp.exp(-gate)) * upward).astype(jnp.bfloat16)
    for step in range(DOWN_STEPS):
        finish(HIDDEN_STEPS + step)
        for shard in range(step * wide, (step + 1) * wide):
            produced = lax.dot_general(
                activated[...],
                down_ref[:, shard * columns : (shard + 1) * columns],
                (((0,), (0,)), ((), ())),
                preferred_element_type=jnp.float32,
            )
            out_ref[shard * blocks : (shard + 1) * blocks] = produced.astype(jnp.bfloat16).reshape(
                blocks, rows // blocks, columns
            )


def expert_rows(core, own, partner, gain, gate, up, down):
    hidden, width = gate.shape
    count, slots, columns = own.shape
    rows = 2 * count * slots * columns // width
    vmem = pl.BlockSpec(memory_space=pltpu.VMEM)
    hbm = pl.BlockSpec(memory_space=pl.ANY)
    return pl.pallas_call(
        experts_kernel,
        out_shape=jax.ShapeDtypeStruct((2 * count, slots, columns), jnp.bfloat16),
        in_specs=[pl.BlockSpec(memory_space=pltpu.SMEM), vmem, vmem, vmem, hbm, hbm, hbm],
        out_specs=vmem,
        scratch_shapes=[
            pltpu.VMEM((rows, width), jnp.bfloat16),
            pltpu.VMEM((hidden, width), jnp.bfloat16),
            pltpu.VMEM((hidden, width), jnp.bfloat16),
            pltpu.VMEM((hidden, width), jnp.bfloat16),
            pltpu.VMEM((hidden, rows), jnp.bfloat16),
            pltpu.SemaphoreType.DMA((HIDDEN_STEPS + DOWN_STEPS, 2)),
        ],
        compiler_params=pltpu.CompilerParams(vmem_limit_bytes=48 * 2**20),
        cost_estimate=pl.CostEstimate(flops=6 * rows * hidden * width, bytes_accessed=6 * hidden * width, transcendentals=0),
        name="experts",
    )(core, own, partner, gain, in_hbm(gate), in_hbm(up), in_hbm(down))


def body(
    query_in,
    key_in,
    value_in,
    decay_rate,
    states,
    attn_gain,
    out_proj,
    stream_in,
    ffn_gain,
    expert_gate,
    expert_up,
    expert_down,
    routes,
    route_weights,
):
    requests_here, positions, width_here = query_in.shape
    groups = lax.axis_size("grp")
    heads = lax.axis_size("head")
    tokens_here = stream_in.shape[0] * positions
    columns = stream_in.shape[2]
    experts = heads * expert_gate.shape[0]
    slots_all = experts * CAP
    attended, picker, combiner, stream, gain, *state_parts = attend(
        query_in, key_in, value_in, decay_rate, attn_gain, routes, route_weights, stream_in, ffn_gain, states, slots_all
    )
    place = lax.axis_index("grp")
    partner = lax.ppermute(attended, "grp", [(one, one ^ 1) for one in range(groups)])
    pair = jnp.where(
        place % 2 == 0, jnp.concatenate([attended, partner]), jnp.concatenate([partner, attended])
    )
    gathered = [pair] + [
        lax.ppermute(pair, "grp", [(one, one ^ (2 * step)) for one in range(groups)]) for step in PLACES[1:]
    ]
    gathered, memory_state = lax.optimization_barrier((gathered, update(*state_parts)))
    partial_sums = project((place // 2).astype(jnp.int32).reshape(1), gathered, out_proj, heads)
    shares = lax.all_to_all(
        partial_sums,
        "head",
        split_axis=0,
        concat_axis=0,
        axis_index_groups=[heads_in_order(heads)],
        tiled=True,
    )
    mixed = jnp.sum(shares.astype(jnp.float32), axis=0)
    residual = (stream + mixed).astype(jnp.bfloat16)
    slot_rows = (
        jnp.dot(picker, residual, preferred_element_type=jnp.float32)
        .astype(jnp.bfloat16)
        .reshape(1, experts, CAP, columns)
    )
    in_order = heads_in_order(heads)
    own = lax.all_to_all(
        jnp.broadcast_to(slot_rows, (groups // 2, experts, CAP, columns)).reshape(-1, CAP, columns),
        ("grp", "head"),
        split_axis=0,
        concat_axis=0,
        axis_index_groups=[
            [(2 * one + core) * heads + head for one in places_in_order(groups // 2) for head in in_order]
            for core in range(2)
        ],
        tiled=True,
    )
    outgoing = expert_rows(
        (place % 2).astype(jnp.int32).reshape(1),
        own,
        lax.ppermute(own, "grp", [(one, one ^ 1) for one in range(groups)]),
        gain,
        expert_gate[0],
        expert_up[0],
        expert_down[0],
    )
    returned = lax.all_to_all(
        outgoing,
        ("grp", "head"),
        split_axis=0,
        concat_axis=0,
        axis_index_groups=[[one * heads + head for one in range(groups) for head in in_order]],
        tiled=True,
    ).reshape(groups, slots_all, columns)
    moe = jnp.dot(
        combiner,
        jnp.sum(returned.astype(jnp.float32), axis=0),
        precision=lax.Precision.HIGHEST,
        preferred_element_type=jnp.float32,
    )
    stream_out = (residual.astype(jnp.float32) + moe).astype(jnp.bfloat16).reshape(stream_in.shape)
    return (stream_out, memory_state)


def solution(mesh):
    return jax.shard_map(
        body,
        mesh=mesh,
        in_specs=(
            P("grp", None, "head"),
            P("grp", None, "head"),
            P("grp", None, "head"),
            P("head"),
            P("grp", "head", None, None),
            P("head"),
            P("head", "grp"),
            P("head", None, "grp"),
            P(),
            P("head", "grp", None),
            P("head", "grp", None),
            P("head", "grp", None),
            P("head", None, None),
            P("head", None, None),
        ),
        out_specs=(P("head", None, "grp"), P("grp", "head", None, None)),
        check_vma=False,
    )
```

```python
import jax
import jax.numpy as jnp
from jax import lax
from jax.experimental import pallas as pl
from jax.experimental.pallas import tpu as pltpu
from jax.sharding import PartitionSpec as P

CAP = 2
PLACES = (0, 1, 3, 2)
LATE_HEAD = 15
FIRST_HEAD = 15
FIRST_PLACE = 3
HIDDEN_STEPS = 4
DOWN_WIDTHS = (3, 3, 2)
TOGETHER = 2
AHEAD = 4


EPSILON = 1e-06


def in_hbm(array):
    return pltpu.with_memory_space_constraint(array, pltpu.HBM)


def heads_in_order(count, first=FIRST_HEAD):
    return [first] + [head for head in range(count) if head != first]


def places_in_order(count):
    return [FIRST_PLACE] + [place for place in range(count) if place != FIRST_PLACE]


ROWS_CONTRACT = (((1,), (1,)), ((), ()))


def attend_kernel(
    query_in, key_in, value_in, decay_in, gain_in, routes_in, weights_in, stream_in, ffn_gain_in, states_in,
    out_ref, picker_ref, combiner_ref, stream_out, ffn_gain_out, held, left, right, faded_twice,
    query_ref, key_ref, value_ref, decay_ref, gain_ref, routes_ref, weights_ref, stream_ref, read, rows, small_sems, in_sems,
):
    requests, positions, _ = query_ref.shape
    heads, size = held.shape[1], held.shape[2]
    pairs = (
        (query_in, query_ref),
        (key_in, key_ref),
        (value_in, value_ref),
        (decay_in, decay_ref),
        (gain_in, gain_ref),
        (routes_in, routes_ref),
        (weights_in, weights_ref),
        (stream_in, stream_ref),
        (ffn_gain_in, ffn_gain_out),
    )
    small = [
        pltpu.make_async_copy(source, target, small_sems.at[index]) for index, (source, target) in enumerate(pairs)
    ]
    arriving = [
        pltpu.make_async_copy(
            states_in.at[pl.ds(start, TOGETHER)], held.at[pl.ds(start, TOGETHER)], in_sems.at[start // TOGETHER]
        )
        for start in range(0, requests, TOGETHER)
    ]
    arriving[0].start()
    for copy in small[:4]:
        copy.start()
    for copy in arriving[1:]:
        copy.start()
    for copy in small[4:]:
        copy.start()
    for copy in small[:4]:
        copy.wait()

    first_part, own_part = [], []
    for head in range(heads):
        columns = slice(head * size, (head + 1) * size)
        query = query_ref[:, :, columns].astype(jnp.float32)
        keys = key_ref[:, :, columns].astype(jnp.float32)
        values = value_ref[:, :, columns].astype(jnp.float32)
        first_key, first_value = keys[:, 0:1, :], values[:, 0:1, :]
        first_part.append(jnp.sum(query * first_key, axis=2, keepdims=True) * first_value)
        own_part.append(jnp.sum(query * keys, axis=2, keepdims=True) * values)
        faded = decay_ref[head] * first_value
        faded_twice[:, columns] = jnp.full((1, size), decay_ref[head] * decay_ref[head], jnp.float32)
        high = faded.astype(jnp.bfloat16).astype(jnp.float32)
        middle = (faded - high).astype(jnp.bfloat16).astype(jnp.float32)
        left[:, :, columns] = jnp.concatenate([first_key, first_key, first_key, keys[:, 1:2, :]], axis=1)
        right[:, :, columns] = jnp.concatenate([high, middle, faded - high - middle, values[:, 1:2, :]], axis=1)

    for request in range(requests):
        if request % TOGETHER == 0:
            arriving[request // TOGETHER].wait()
        for head in range(heads):
            columns = slice(head * size, (head + 1) * size)
            state = held[request, head]
            high = state.astype(jnp.bfloat16)
            low = (state - high.astype(jnp.float32)).astype(jnp.bfloat16)
            query = query_ref[request, :, columns]
            read[request, :, columns] = jnp.dot(
                jnp.concatenate([query, query], axis=1),
                jnp.concatenate([high, low], axis=0),
                preferred_element_type=jnp.float32,
            )

    for copy in small[4:]:
        copy.wait()
    first = lax.broadcasted_iota(jnp.int32, (requests, positions, size), 1) == 0
    for head in range(heads):
        columns = slice(head * size, (head + 1) * size)
        decay = decay_ref[head]
        once = decay * read[:, :, columns] + first_part[head]
        readout = jnp.where(first, once, decay * once + own_part[head])
        scaled = (
            readout
            * lax.rsqrt(jnp.mean(readout * readout, axis=2, keepdims=True) + EPSILON)
            * gain_ref[0:1, columns][None]
        )
        for request in range(requests):
            rows[request * positions : (request + 1) * positions, columns] = scaled[request]
    out_ref[...] = rows[...].astype(jnp.bfloat16)

    token_count, choices = picker_ref.shape[1], routes_ref.shape[1]
    chosen, weights = [], []
    for token in range(token_count):
        for choice in range(choices):
            place = (token % positions, choice, token // positions)
            chosen.append(routes_ref[place])
            weights.append(weights_ref[place])
    slot_down = lax.broadcasted_iota(jnp.int32, picker_ref.shape, 0)
    token_across = lax.broadcasted_iota(jnp.int32, picker_ref.shape, 1)
    token_down = lax.broadcasted_iota(jnp.int32, combiner_ref.shape, 0)
    slot_across = lax.broadcasted_iota(jnp.int32, combiner_ref.shape, 1)
    picker = jnp.zeros(picker_ref.shape, jnp.float32)
    combiner = jnp.zeros(combiner_ref.shape, jnp.float32)
    for index, expert in enumerate(chosen):
        position = jnp.where(expert == FIRST_HEAD, 0, expert + (expert < FIRST_HEAD).astype(jnp.int32))
        slot = position * CAP
        for earlier in chosen[:index]:
            slot = slot + (earlier == expert).astype(jnp.int32)
        token = index // choices
        picker = jnp.where((slot_down == slot) & (token_across == token), 1.0, picker)
        combiner = jnp.where((slot_across == slot) & (token_down == token), weights[index], combiner)
    picker_ref[...] = picker.astype(jnp.bfloat16)
    combiner_ref[...] = combiner
    stream_out[...] = stream_ref[...].astype(jnp.float32).reshape(stream_out.shape)


def attend(
    query_in, key_in, value_in, decay_rate, attn_gain, routes, route_weights, stream_in, ffn_gain, states, slots
):
    requests, positions, width = query_in.shape
    tokens = stream_in.shape[0] * stream_in.shape[1]
    routes, route_weights = (jnp.transpose(array, (1, 2, 0)) for array in (routes, route_weights))
    vmem = pl.BlockSpec(memory_space=pltpu.VMEM)
    anywhere = pl.BlockSpec(memory_space=pl.ANY)
    inputs = (
        query_in, key_in, value_in, decay_rate, attn_gain.reshape(1, width), routes, route_weights, stream_in,
        ffn_gain.reshape(1, -1), states,
    )
    return pl.pallas_call(
        attend_kernel,
        out_shape=[
            pltpu.VMEM((requests * positions, width), jnp.bfloat16),
            pltpu.VMEM((slots, tokens), jnp.bfloat16),
            pltpu.VMEM((tokens, slots), jnp.float32),
            pltpu.VMEM((tokens, stream_in.shape[2]), jnp.float32),
            pltpu.VMEM((1, ffn_gain.shape[0]), jnp.float32),
            pltpu.VMEM(states.shape, jnp.float32),
            pltpu.VMEM((requests, 4, width), jnp.float32),
            pltpu.VMEM((requests, 4, width), jnp.float32),
            pltpu.VMEM((1, width), jnp.float32),
        ],
        in_specs=[anywhere] * len(inputs),
        out_specs=[vmem] * 9,
        scratch_shapes=[
            pltpu.VMEM(query_in.shape, jnp.bfloat16),
            pltpu.VMEM(query_in.shape, jnp.bfloat16),
            pltpu.VMEM(query_in.shape, jnp.bfloat16),
            pltpu.SMEM(decay_rate.shape, jnp.float32),
            pltpu.VMEM((1, width), jnp.float32),
            pltpu.SMEM(routes.shape, jnp.int32),
            pltpu.SMEM(route_weights.shape, jnp.float32),
            pltpu.VMEM(stream_in.shape, jnp.bfloat16),
            pltpu.VMEM(query_in.shape, jnp.float32),
            pltpu.VMEM((requests * positions, width), jnp.float32),
            pltpu.SemaphoreType.DMA((9,)),
            pltpu.SemaphoreType.DMA((requests,)),
        ],
        compiler_params=pltpu.CompilerParams(vmem_limit_bytes=32 * 2**20),
        cost_estimate=pl.CostEstimate(flops=10**7, bytes_accessed=states.size * 4, transcendentals=0),
        name="attend",
    )(*(in_hbm(array) for array in inputs))


def project_kernel(place_ref, own_ref, second_ref, third_ref, fourth_ref, weights_ref, out_ref, everyone):
    place = place_ref[0]
    rows = own_ref.shape[0]
    blocks, each, _ = out_ref.shape
    for index, ref in zip(PLACES, (own_ref, second_ref, third_ref, fourth_ref)):
        everyone[pl.ds(pl.multiple_of((place ^ index) * rows, rows), rows), :] = ref[...]
    partial = jnp.dot(everyone[...], weights_ref[...], preferred_element_type=jnp.float32).astype(jnp.bfloat16)
    for position, block in enumerate(heads_in_order(blocks, LATE_HEAD)):
        out_ref[position] = partial[block * each : (block + 1) * each]


def project(place, gathered, weights, blocks):
    rows = len(gathered) * gathered[0].shape[0]
    vmem = pl.BlockSpec(memory_space=pltpu.VMEM)
    return pl.pallas_call(
        project_kernel,
        out_shape=jax.ShapeDtypeStruct((blocks, rows // blocks, weights.shape[1]), jnp.bfloat16),
        in_specs=[pl.BlockSpec(memory_space=pltpu.SMEM)] + [vmem] * 5,
        out_specs=vmem,
        scratch_shapes=[pltpu.VMEM((rows, weights.shape[0]), jnp.bfloat16)],
        compiler_params=pltpu.CompilerParams(vmem_limit_bytes=8 * 2**20),
        cost_estimate=pl.CostEstimate(flops=2 * rows * weights.size, bytes_accessed=2 * weights.size, transcendentals=0),
        name="project",
    )(place, *gathered, weights)


def update_kernel(states_ref, left_ref, right_ref, faded_ref, states_out, updated, sems):
    requests, heads, size, _ = states_ref.shape
    leaving = []
    for request in range(requests):
        for head in range(heads):
            columns = slice(head * size, (head + 1) * size)
            added = lax.dot_general(
                left_ref[request, :, columns].astype(jnp.bfloat16),
                right_ref[request, :, columns].astype(jnp.bfloat16),
                (((0,), (0,)), ((), ())),
                preferred_element_type=jnp.float32,
            )
            updated[request, head] = faded_ref[:, columns] * states_ref[request, head] + added
        leaving.append(pltpu.make_async_copy(updated.at[request], states_out.at[request], sems.at[request]))
        leaving[-1].start()
    for copy in leaving:
        copy.wait()


def update(states, left, right, faded_twice):
    vmem = pl.BlockSpec(memory_space=pltpu.VMEM)
    return pl.pallas_call(
        update_kernel,
        out_shape=pltpu.HBM(states.shape, jnp.float32),
        in_specs=[vmem] * 4,
        out_specs=pl.BlockSpec(memory_space=pl.ANY),
        scratch_shapes=[pltpu.VMEM(states.shape, jnp.float32), pltpu.SemaphoreType.DMA((states.shape[0],))],
        compiler_params=pltpu.CompilerParams(vmem_limit_bytes=16 * 2**20),
        cost_estimate=pl.CostEstimate(flops=10**7, bytes_accessed=states.size * 4, transcendentals=0),
        name="update",
    )(states, left, right, faded_twice)


def experts_kernel(
    core_ref, own_ref, partner_ref, gain_ref, gate_in, up_in, down_in, out_ref,
    normed, gate_ref, up_ref, down_ref, activated, sems,
):
    hidden, width = gate_in.shape
    columns = own_ref.shape[2]
    shards = width // columns
    places = places_in_order(shards // 2)
    blocks = own_ref.shape[0] // len(places)
    rows = blocks * own_ref.shape[1]
    tile = hidden // HIDDEN_STEPS
    steps = HIDDEN_STEPS + len(DOWN_WIDTHS)

    def down_shards(step):
        start = sum(DOWN_WIDTHS[:step])
        return range(start, start + DOWN_WIDTHS[step])

    def copies(step):
        if step < HIDDEN_STEPS:
            cut = pl.ds(step * tile, tile)
            parts = [(gate_in.at[cut], gate_ref.at[cut]), (up_in.at[cut], up_ref.at[cut])]
        else:
            here = down_shards(step - HIDDEN_STEPS)
            cut = pl.ds(here.start * columns, len(here) * columns)
            parts = [(down_in.at[:, cut], down_ref.at[:, cut])]
        return [
            pltpu.make_async_copy(source, target, sems.at[step, index])
            for index, (source, target) in enumerate(parts)
        ]

    def begin(step):
        if step < steps:
            for copy in copies(step):
                copy.start()

    def finish(step):
        for copy in copies(step):
            copy.wait()
        begin(step + AHEAD)

    for step in range(AHEAD):
        begin(step)
    core = core_ref[0]
    squares = jnp.zeros((rows, 1), jnp.float32)
    for ref, side in ((own_ref, core), (partner_ref, 1 - core)):
        for index, place in enumerate(places):
            arrived = ref[index * blocks : (index + 1) * blocks].reshape(rows, columns)
            normed[:, pl.ds(pl.multiple_of((2 * place + side) * columns, 128), columns)] = arrived
            arrived = arrived.astype(jnp.float32)
            squares = squares + jnp.sum(arrived * arrived, axis=1, keepdims=True)
    scale = lax.rsqrt(squares / width + EPSILON)
    for shard in range(shards):
        cut = slice(shard * columns, (shard + 1) * columns)
        normed[:, cut] = (normed[:, cut].astype(jnp.float32) * scale * gain_ref[:, cut]).astype(jnp.bfloat16)
    for step in range(HIDDEN_STEPS):
        finish(step)
        cut = slice(step * tile, (step + 1) * tile)
        gate = lax.dot_general(gate_ref[cut], normed[...], ROWS_CONTRACT, preferred_element_type=jnp.float32)
        upward = lax.dot_general(up_ref[cut], normed[...], ROWS_CONTRACT, preferred_element_type=jnp.float32)
        activated[cut, :] = (gate / (1.0 + jnp.exp(-gate)) * upward).astype(jnp.bfloat16)
    for step in range(len(DOWN_WIDTHS)):
        finish(HIDDEN_STEPS + step)
        for shard in down_shards(step):
            produced = lax.dot_general(
                activated[...],
                down_ref[:, shard * columns : (shard + 1) * columns],
                (((0,), (0,)), ((), ())),
                preferred_element_type=jnp.float32,
            )
            out_ref[shard * blocks : (shard + 1) * blocks] = produced.astype(jnp.bfloat16).reshape(
                blocks, rows // blocks, columns
            )


def expert_rows(core, own, partner, gain, gate, up, down):
    hidden, width = gate.shape
    count, slots, columns = own.shape
    rows = 2 * count * slots * columns // width
    vmem = pl.BlockSpec(memory_space=pltpu.VMEM)
    hbm = pl.BlockSpec(memory_space=pl.ANY)
    return pl.pallas_call(
        experts_kernel,
        out_shape=jax.ShapeDtypeStruct((2 * count, slots, columns), jnp.bfloat16),
        in_specs=[pl.BlockSpec(memory_space=pltpu.SMEM), vmem, vmem, vmem, hbm, hbm, hbm],
        out_specs=vmem,
        scratch_shapes=[
            pltpu.VMEM((rows, width), jnp.bfloat16),
            pltpu.VMEM((hidden, width), jnp.bfloat16),
            pltpu.VMEM((hidden, width), jnp.bfloat16),
            pltpu.VMEM((hidden, width), jnp.bfloat16),
            pltpu.VMEM((hidden, rows), jnp.bfloat16),
            pltpu.SemaphoreType.DMA((HIDDEN_STEPS + len(DOWN_WIDTHS), 2)),
        ],
        compiler_params=pltpu.CompilerParams(vmem_limit_bytes=48 * 2**20),
        cost_estimate=pl.CostEstimate(flops=6 * rows * hidden * width, bytes_accessed=6 * hidden * width, transcendentals=0),
        name="experts",
    )(core, own, partner, gain, in_hbm(gate), in_hbm(up), in_hbm(down))


def body(
    query_in,
    key_in,
    value_in,
    decay_rate,
    states,
    attn_gain,
    out_proj,
    stream_in,
    ffn_gain,
    expert_gate,
    expert_up,
    expert_down,
    routes,
    route_weights,
):
    requests_here, positions, width_here = query_in.shape
    groups = lax.axis_size("grp")
    heads = lax.axis_size("head")
    tokens_here = stream_in.shape[0] * positions
    columns = stream_in.shape[2]
    experts = heads * expert_gate.shape[0]
    slots_all = experts * CAP
    attended, picker, combiner, stream, gain, *state_parts = attend(
        query_in, key_in, value_in, decay_rate, attn_gain, routes, route_weights, stream_in, ffn_gain, states, slots_all
    )
    place = lax.axis_index("grp")
    partner = lax.ppermute(attended, "grp", [(one, one ^ 1) for one in range(groups)])
    pair = jnp.where(
        place % 2 == 0, jnp.concatenate([attended, partner]), jnp.concatenate([partner, attended])
    )
    gathered = [pair] + [
        lax.ppermute(pair, "grp", [(one, one ^ (2 * step)) for one in range(groups)]) for step in PLACES[1:]
    ]
    gathered, memory_state = lax.optimization_barrier((gathered, update(*state_parts)))
    partial_sums = project((place // 2).astype(jnp.int32).reshape(1), gathered, out_proj, heads)
    shares = lax.all_to_all(
        partial_sums,
        "head",
        split_axis=0,
        concat_axis=0,
        axis_index_groups=[heads_in_order(heads, LATE_HEAD)],
        tiled=True,
    )
    mixed = jnp.sum(shares.astype(jnp.float32), axis=0)
    residual = (stream + mixed).astype(jnp.bfloat16)
    slot_rows = (
        jnp.dot(picker, residual, preferred_element_type=jnp.float32)
        .astype(jnp.bfloat16)
        .reshape(1, experts, CAP, columns)
    )
    in_order = heads_in_order(heads)
    own = lax.all_to_all(
        jnp.broadcast_to(slot_rows, (groups // 2, experts, CAP, columns)).reshape(-1, CAP, columns),
        ("grp", "head"),
        split_axis=0,
        concat_axis=0,
        axis_index_groups=[
            [(2 * one + core) * heads + head for one in places_in_order(groups // 2) for head in in_order]
            for core in range(2)
        ],
        tiled=True,
    )
    outgoing = expert_rows(
        (place % 2).astype(jnp.int32).reshape(1),
        own,
        lax.ppermute(own, "grp", [(one, one ^ 1) for one in range(groups)]),
        gain,
        expert_gate[0],
        expert_up[0],
        expert_down[0],
    )
    returned = lax.all_to_all(
        outgoing,
        ("grp", "head"),
        split_axis=0,
        concat_axis=0,
        axis_index_groups=[[one * heads + head for one in range(groups) for head in in_order]],
        tiled=True,
    ).reshape(groups, slots_all, columns)
    moe = jnp.dot(
        combiner,
        jnp.sum(returned.astype(jnp.float32), axis=0),
        precision=lax.Precision.HIGHEST,
        preferred_element_type=jnp.float32,
    )
    stream_out = (residual.astype(jnp.float32) + moe).astype(jnp.bfloat16).reshape(stream_in.shape)
    return (stream_out, memory_state)


def solution(mesh):
    return jax.shard_map(
        body,
        mesh=mesh,
        in_specs=(
            P("grp", None, "head"),
            P("grp", None, "head"),
            P("grp", None, "head"),
            P("head"),
            P("grp", "head", None, None),
            P("head"),
            P("head", "grp"),
            P("head", None, "grp"),
            P(),
            P("head", "grp", None),
            P("head", "grp", None),
            P("head", "grp", None),
            P("head", None, None),
            P("head", None, None),
        ),
        out_specs=(P("head", None, "grp"), P("grp", "head", None, None)),
        check_vma=False,
    )
```

```python
import jax
import jax.numpy as jnp
from jax import lax
from jax.experimental import pallas as pl
from jax.experimental.pallas import tpu as pltpu
from jax.sharding import PartitionSpec as P

CAP = 2
PLACES = (0, 1, 3, 2)
LATE_HEAD = 15
FIRST_HEAD = 15
FIRST_PLACE = 3
LEAD = 64
HIDDEN_STEPS = 4
DOWN_WIDTHS = (3, 3, 2)
TOGETHER = 2
AHEAD = 4


EPSILON = 1e-06


def in_hbm(array):
    return pltpu.with_memory_space_constraint(array, pltpu.HBM)


def heads_in_order(count, first=FIRST_HEAD):
    return [first] + [head for head in range(count) if head != first]


def places_in_order(count):
    return [FIRST_PLACE] + [place for place in range(count) if place != FIRST_PLACE]


ROWS_CONTRACT = (((1,), (1,)), ((), ()))


def attend_kernel(
    query_in, key_in, value_in, decay_in, gain_in, routes_in, weights_in, stream_in, ffn_gain_in, states_in,
    out_ref, picker_ref, combiner_ref, stream_out, ffn_gain_out, held, left, right, faded_twice,
    query_ref, key_ref, value_ref, decay_ref, gain_ref, routes_ref, weights_ref, stream_ref, read, rows, small_sems, in_sems,
):
    requests, positions, _ = query_ref.shape
    heads, size = held.shape[1], held.shape[2]
    pairs = (
        (query_in, query_ref),
        (key_in, key_ref),
        (value_in, value_ref),
        (decay_in, decay_ref),
        (gain_in, gain_ref),
        (routes_in, routes_ref),
        (weights_in, weights_ref),
        (stream_in, stream_ref),
        (ffn_gain_in, ffn_gain_out),
    )
    small = [
        pltpu.make_async_copy(source, target, small_sems.at[index]) for index, (source, target) in enumerate(pairs)
    ]
    arriving = [
        pltpu.make_async_copy(
            states_in.at[pl.ds(start, TOGETHER)], held.at[pl.ds(start, TOGETHER)], in_sems.at[start // TOGETHER]
        )
        for start in range(0, requests, TOGETHER)
    ]
    arriving[0].start()
    for copy in small[:4]:
        copy.start()
    for copy in arriving[1:]:
        copy.start()
    for copy in small[4:]:
        copy.start()
    for copy in small[:4]:
        copy.wait()

    first_part, own_part = [], []
    for head in range(heads):
        columns = slice(head * size, (head + 1) * size)
        query = query_ref[:, :, columns].astype(jnp.float32)
        keys = key_ref[:, :, columns].astype(jnp.float32)
        values = value_ref[:, :, columns].astype(jnp.float32)
        first_key, first_value = keys[:, 0:1, :], values[:, 0:1, :]
        first_part.append(jnp.sum(query * first_key, axis=2, keepdims=True) * first_value)
        own_part.append(jnp.sum(query * keys, axis=2, keepdims=True) * values)
        faded = decay_ref[head] * first_value
        faded_twice[:, columns] = jnp.full((1, size), decay_ref[head] * decay_ref[head], jnp.float32)
        high = faded.astype(jnp.bfloat16).astype(jnp.float32)
        middle = (faded - high).astype(jnp.bfloat16).astype(jnp.float32)
        left[:, :, columns] = jnp.concatenate([first_key, first_key, first_key, keys[:, 1:2, :]], axis=1)
        right[:, :, columns] = jnp.concatenate([high, middle, faded - high - middle, values[:, 1:2, :]], axis=1)

    for request in range(requests):
        if request % TOGETHER == 0:
            arriving[request // TOGETHER].wait()
        for head in range(heads):
            columns = slice(head * size, (head + 1) * size)
            state = held[request, head]
            high = state.astype(jnp.bfloat16)
            low = (state - high.astype(jnp.float32)).astype(jnp.bfloat16)
            query = query_ref[request, :, columns]
            read[request, :, columns] = jnp.dot(
                jnp.concatenate([query, query], axis=1),
                jnp.concatenate([high, low], axis=0),
                preferred_element_type=jnp.float32,
            )

    for copy in small[4:]:
        copy.wait()
    first = lax.broadcasted_iota(jnp.int32, (requests, positions, size), 1) == 0
    for head in range(heads):
        columns = slice(head * size, (head + 1) * size)
        decay = decay_ref[head]
        once = decay * read[:, :, columns] + first_part[head]
        readout = jnp.where(first, once, decay * once + own_part[head])
        scaled = (
            readout
            * lax.rsqrt(jnp.mean(readout * readout, axis=2, keepdims=True) + EPSILON)
            * gain_ref[0:1, columns][None]
        )
        for request in range(requests):
            rows[request * positions : (request + 1) * positions, columns] = scaled[request]
    out_ref[...] = rows[...].astype(jnp.bfloat16)

    token_count, choices = picker_ref.shape[1], routes_ref.shape[1]
    chosen, weights = [], []
    for token in range(token_count):
        for choice in range(choices):
            place = (token % positions, choice, token // positions)
            chosen.append(routes_ref[place])
            weights.append(weights_ref[place])
    slot_down = lax.broadcasted_iota(jnp.int32, picker_ref.shape, 0)
    token_across = lax.broadcasted_iota(jnp.int32, picker_ref.shape, 1)
    token_down = lax.broadcasted_iota(jnp.int32, combiner_ref.shape, 0)
    slot_across = lax.broadcasted_iota(jnp.int32, combiner_ref.shape, 1)
    picker = jnp.zeros(picker_ref.shape, jnp.float32)
    combiner = jnp.zeros(combiner_ref.shape, jnp.float32)
    for index, expert in enumerate(chosen):
        position = jnp.where(expert == FIRST_HEAD, 0, expert + (expert < FIRST_HEAD).astype(jnp.int32))
        slot = position * CAP
        for earlier in chosen[:index]:
            slot = slot + (earlier == expert).astype(jnp.int32)
        token = index // choices
        picker = jnp.where((slot_down == slot) & (token_across == token), 1.0, picker)
        combiner = jnp.where((slot_across == slot) & (token_down == token), weights[index], combiner)
    picker_ref[...] = picker.astype(jnp.bfloat16)
    combiner_ref[...] = combiner
    stream_out[...] = stream_ref[...].astype(jnp.float32).reshape(stream_out.shape)


def attend(
    query_in, key_in, value_in, decay_rate, attn_gain, routes, route_weights, stream_in, ffn_gain, states, slots
):
    requests, positions, width = query_in.shape
    tokens = stream_in.shape[0] * stream_in.shape[1]
    routes, route_weights = (jnp.transpose(array, (1, 2, 0)) for array in (routes, route_weights))
    vmem = pl.BlockSpec(memory_space=pltpu.VMEM)
    anywhere = pl.BlockSpec(memory_space=pl.ANY)
    inputs = (
        query_in, key_in, value_in, decay_rate, attn_gain.reshape(1, width), routes, route_weights, stream_in,
        ffn_gain.reshape(1, -1), states,
    )
    return pl.pallas_call(
        attend_kernel,
        out_shape=[
            pltpu.VMEM((requests * positions, width), jnp.bfloat16),
            pltpu.VMEM((slots, tokens), jnp.bfloat16),
            pltpu.VMEM((tokens, slots), jnp.float32),
            pltpu.VMEM((tokens, stream_in.shape[2]), jnp.float32),
            pltpu.VMEM((1, ffn_gain.shape[0]), jnp.float32),
            pltpu.VMEM(states.shape, jnp.float32),
            pltpu.VMEM((requests, 4, width), jnp.float32),
            pltpu.VMEM((requests, 4, width), jnp.float32),
            pltpu.VMEM((1, width), jnp.float32),
        ],
        in_specs=[anywhere] * len(inputs),
        out_specs=[vmem] * 9,
        scratch_shapes=[
            pltpu.VMEM(query_in.shape, jnp.bfloat16),
            pltpu.VMEM(query_in.shape, jnp.bfloat16),
            pltpu.VMEM(query_in.shape, jnp.bfloat16),
            pltpu.SMEM(decay_rate.shape, jnp.float32),
            pltpu.VMEM((1, width), jnp.float32),
            pltpu.SMEM(routes.shape, jnp.int32),
            pltpu.SMEM(route_weights.shape, jnp.float32),
            pltpu.VMEM(stream_in.shape, jnp.bfloat16),
            pltpu.VMEM(query_in.shape, jnp.float32),
            pltpu.VMEM((requests * positions, width), jnp.float32),
            pltpu.SemaphoreType.DMA((9,)),
            pltpu.SemaphoreType.DMA((requests,)),
        ],
        compiler_params=pltpu.CompilerParams(vmem_limit_bytes=32 * 2**20),
        cost_estimate=pl.CostEstimate(flops=10**7, bytes_accessed=states.size * 4, transcendentals=0),
        name="attend",
    )(*(in_hbm(array) for array in inputs))


def project_kernel(place_ref, own_ref, second_ref, third_ref, fourth_ref, weights_ref, out_ref, everyone):
    place = place_ref[0]
    rows = own_ref.shape[0]
    blocks, each, _ = out_ref.shape
    for index, ref in zip(PLACES, (own_ref, second_ref, third_ref, fourth_ref)):
        everyone[pl.ds(pl.multiple_of((place ^ index) * rows, rows), rows), :] = ref[...]
    partial = jnp.dot(everyone[...], weights_ref[...], preferred_element_type=jnp.float32).astype(jnp.bfloat16)
    for position, block in enumerate(heads_in_order(blocks, LATE_HEAD)):
        out_ref[position] = partial[block * each : (block + 1) * each]


def project(place, gathered, weights, blocks):
    rows = len(gathered) * gathered[0].shape[0]
    vmem = pl.BlockSpec(memory_space=pltpu.VMEM)
    return pl.pallas_call(
        project_kernel,
        out_shape=jax.ShapeDtypeStruct((blocks, rows // blocks, weights.shape[1]), jnp.bfloat16),
        in_specs=[pl.BlockSpec(memory_space=pltpu.SMEM)] + [vmem] * 5,
        out_specs=vmem,
        scratch_shapes=[pltpu.VMEM((rows, weights.shape[0]), jnp.bfloat16)],
        compiler_params=pltpu.CompilerParams(vmem_limit_bytes=8 * 2**20),
        cost_estimate=pl.CostEstimate(flops=2 * rows * weights.size, bytes_accessed=2 * weights.size, transcendentals=0),
        name="project",
    )(place, *gathered, weights)


def update_kernel(states_ref, left_ref, right_ref, faded_ref, states_out, updated, sems):
    requests, heads, size, _ = states_ref.shape
    leaving = []
    for request in range(requests):
        for head in range(heads):
            columns = slice(head * size, (head + 1) * size)
            added = lax.dot_general(
                left_ref[request, :, columns].astype(jnp.bfloat16),
                right_ref[request, :, columns].astype(jnp.bfloat16),
                (((0,), (0,)), ((), ())),
                preferred_element_type=jnp.float32,
            )
            updated[request, head] = faded_ref[:, columns] * states_ref[request, head] + added
        leaving.append(pltpu.make_async_copy(updated.at[request], states_out.at[request], sems.at[request]))
        leaving[-1].start()
    for copy in leaving:
        copy.wait()


def update(states, left, right, faded_twice):
    vmem = pl.BlockSpec(memory_space=pltpu.VMEM)
    return pl.pallas_call(
        update_kernel,
        out_shape=pltpu.HBM(states.shape, jnp.float32),
        in_specs=[vmem] * 4,
        out_specs=pl.BlockSpec(memory_space=pl.ANY),
        scratch_shapes=[pltpu.VMEM(states.shape, jnp.float32), pltpu.SemaphoreType.DMA((states.shape[0],))],
        compiler_params=pltpu.CompilerParams(vmem_limit_bytes=16 * 2**20),
        cost_estimate=pl.CostEstimate(flops=10**7, bytes_accessed=states.size * 4, transcendentals=0),
        name="update",
    )(states, left, right, faded_twice)


def lead_kernel(gate_in, up_in, gate_first, up_first, sems):
    lead = gate_first.shape[0]
    copies = [
        pltpu.make_async_copy(source.at[pl.ds(0, lead)], target, sems.at[index])
        for index, (source, target) in enumerate(((gate_in, gate_first), (up_in, up_first)))
    ]
    for copy in copies:
        copy.start()
    for copy in copies:
        copy.wait()


def lead_rows(gate, up):
    anywhere = pl.BlockSpec(memory_space=pl.ANY)
    first = pltpu.VMEM((LEAD, gate.shape[1]), gate.dtype)
    return pl.pallas_call(
        lead_kernel,
        out_shape=[first, first],
        in_specs=[anywhere] * 2,
        out_specs=[pl.BlockSpec(memory_space=pltpu.VMEM)] * 2,
        scratch_shapes=[pltpu.SemaphoreType.DMA((2,))],
        compiler_params=pltpu.CompilerParams(vmem_limit_bytes=16 * 2**20),
        cost_estimate=pl.CostEstimate(flops=0, bytes_accessed=4 * LEAD * gate.shape[1], transcendentals=0),
        name="lead_rows",
    )(in_hbm(gate), in_hbm(up))


def experts_kernel(
    core_ref, own_ref, partner_ref, gain_ref, gate_first, up_first, gate_in, up_in, down_in, out_ref,
    normed, gate_ref, up_ref, down_ref, activated, sems,
):
    hidden, width = gate_in.shape
    columns = own_ref.shape[2]
    shards = width // columns
    places = places_in_order(shards // 2)
    blocks = own_ref.shape[0] // len(places)
    rows = blocks * own_ref.shape[1]
    lead = gate_first.shape[0]
    tile = (hidden - lead) // HIDDEN_STEPS
    steps = HIDDEN_STEPS + len(DOWN_WIDTHS)

    def down_shards(step):
        start = sum(DOWN_WIDTHS[:step])
        return range(start, start + DOWN_WIDTHS[step])

    def copies(step):
        if step < HIDDEN_STEPS:
            cut = pl.ds(lead + step * tile, tile)
            parts = [(gate_in.at[cut], gate_ref.at[cut]), (up_in.at[cut], up_ref.at[cut])]
        else:
            here = down_shards(step - HIDDEN_STEPS)
            cut = pl.ds(here.start * columns, len(here) * columns)
            parts = [(down_in.at[:, cut], down_ref.at[:, cut])]
        return [
            pltpu.make_async_copy(source, target, sems.at[step, index])
            for index, (source, target) in enumerate(parts)
        ]

    def begin(step):
        if step < steps:
            for copy in copies(step):
                copy.start()

    def finish(step):
        for copy in copies(step):
            copy.wait()
        begin(step + AHEAD)

    for step in range(AHEAD):
        begin(step)
    core = core_ref[0]
    squares = jnp.zeros((rows, 1), jnp.float32)
    for ref, side in ((own_ref, core), (partner_ref, 1 - core)):
        for index, place in enumerate(places):
            arrived = ref[index * blocks : (index + 1) * blocks].reshape(rows, columns)
            normed[:, pl.ds(pl.multiple_of((2 * place + side) * columns, 128), columns)] = arrived
            arrived = arrived.astype(jnp.float32)
            squares = squares + jnp.sum(arrived * arrived, axis=1, keepdims=True)
    scale = lax.rsqrt(squares / width + EPSILON)
    for shard in range(shards):
        cut = slice(shard * columns, (shard + 1) * columns)
        normed[:, cut] = (normed[:, cut].astype(jnp.float32) * scale * gain_ref[:, cut]).astype(jnp.bfloat16)
    def activate(gate_rows, up_rows, cut):
        gate = lax.dot_general(gate_rows, normed[...], ROWS_CONTRACT, preferred_element_type=jnp.float32)
        upward = lax.dot_general(up_rows, normed[...], ROWS_CONTRACT, preferred_element_type=jnp.float32)
        activated[cut, :] = (gate / (1.0 + jnp.exp(-gate)) * upward).astype(jnp.bfloat16)

    activate(gate_first[...], up_first[...], slice(0, lead))
    for step in range(HIDDEN_STEPS):
        finish(step)
        cut = slice(lead + step * tile, lead + (step + 1) * tile)
        activate(gate_ref[cut], up_ref[cut], cut)
    for step in range(len(DOWN_WIDTHS)):
        finish(HIDDEN_STEPS + step)
        for shard in down_shards(step):
            produced = lax.dot_general(
                activated[...],
                down_ref[:, shard * columns : (shard + 1) * columns],
                (((0,), (0,)), ((), ())),
                preferred_element_type=jnp.float32,
            )
            out_ref[shard * blocks : (shard + 1) * blocks] = produced.astype(jnp.bfloat16).reshape(
                blocks, rows // blocks, columns
            )


def expert_rows(core, own, partner, gain, firsts, gate, up, down):
    hidden, width = gate.shape
    count, slots, columns = own.shape
    rows = 2 * count * slots * columns // width
    vmem = pl.BlockSpec(memory_space=pltpu.VMEM)
    hbm = pl.BlockSpec(memory_space=pl.ANY)
    return pl.pallas_call(
        experts_kernel,
        out_shape=jax.ShapeDtypeStruct((2 * count, slots, columns), jnp.bfloat16),
        in_specs=[pl.BlockSpec(memory_space=pltpu.SMEM)] + [vmem] * 5 + [hbm] * 3,
        out_specs=vmem,
        scratch_shapes=[
            pltpu.VMEM((rows, width), jnp.bfloat16),
            pltpu.VMEM((hidden, width), jnp.bfloat16),
            pltpu.VMEM((hidden, width), jnp.bfloat16),
            pltpu.VMEM((hidden, width), jnp.bfloat16),
            pltpu.VMEM((hidden, rows), jnp.bfloat16),
            pltpu.SemaphoreType.DMA((HIDDEN_STEPS + len(DOWN_WIDTHS), 2)),
        ],
        compiler_params=pltpu.CompilerParams(vmem_limit_bytes=48 * 2**20),
        cost_estimate=pl.CostEstimate(flops=6 * rows * hidden * width, bytes_accessed=6 * hidden * width, transcendentals=0),
        name="experts",
    )(core, own, partner, gain, *firsts, in_hbm(gate), in_hbm(up), in_hbm(down))


def body(
    query_in,
    key_in,
    value_in,
    decay_rate,
    states,
    attn_gain,
    out_proj,
    stream_in,
    ffn_gain,
    expert_gate,
    expert_up,
    expert_down,
    routes,
    route_weights,
):
    requests_here, positions, width_here = query_in.shape
    groups = lax.axis_size("grp")
    heads = lax.axis_size("head")
    tokens_here = stream_in.shape[0] * positions
    columns = stream_in.shape[2]
    experts = heads * expert_gate.shape[0]
    slots_all = experts * CAP
    attended, picker, combiner, stream, gain, *state_parts = attend(
        query_in, key_in, value_in, decay_rate, attn_gain, routes, route_weights, stream_in, ffn_gain, states, slots_all
    )
    place = lax.axis_index("grp")
    partner = lax.ppermute(attended, "grp", [(one, one ^ 1) for one in range(groups)])
    pair = jnp.where(
        place % 2 == 0, jnp.concatenate([attended, partner]), jnp.concatenate([partner, attended])
    )
    gathered = [pair] + [
        lax.ppermute(pair, "grp", [(one, one ^ (2 * step)) for one in range(groups)]) for step in PLACES[1:]
    ]
    gathered, memory_state = lax.optimization_barrier((gathered, update(*state_parts)))
    partial_sums = project((place // 2).astype(jnp.int32).reshape(1), gathered, out_proj, heads)
    shares = lax.all_to_all(
        partial_sums,
        "head",
        split_axis=0,
        concat_axis=0,
        axis_index_groups=[heads_in_order(heads, LATE_HEAD)],
        tiled=True,
    )
    mixed = jnp.sum(shares.astype(jnp.float32), axis=0)
    residual = (stream + mixed).astype(jnp.bfloat16)
    slot_rows = (
        jnp.dot(picker, residual, preferred_element_type=jnp.float32)
        .astype(jnp.bfloat16)
        .reshape(1, experts, CAP, columns)
    )
    in_order = heads_in_order(heads)
    own = lax.all_to_all(
        jnp.broadcast_to(slot_rows, (groups // 2, experts, CAP, columns)).reshape(-1, CAP, columns),
        ("grp", "head"),
        split_axis=0,
        concat_axis=0,
        axis_index_groups=[
            [(2 * one + core) * heads + head for one in places_in_order(groups // 2) for head in in_order]
            for core in range(2)
        ],
        tiled=True,
    )
    own, gate_source, up_source = lax.optimization_barrier((own, expert_gate[0], expert_up[0]))
    outgoing = expert_rows(
        (place % 2).astype(jnp.int32).reshape(1),
        own,
        lax.ppermute(own, "grp", [(one, one ^ 1) for one in range(groups)]),
        gain,
        lead_rows(gate_source, up_source),
        expert_gate[0],
        expert_up[0],
        expert_down[0],
    )
    returned = lax.all_to_all(
        outgoing,
        ("grp", "head"),
        split_axis=0,
        concat_axis=0,
        axis_index_groups=[[one * heads + head for one in range(groups) for head in in_order]],
        tiled=True,
    ).reshape(groups, slots_all, columns)
    moe = jnp.dot(
        combiner,
        jnp.sum(returned.astype(jnp.float32), axis=0),
        precision=lax.Precision.HIGHEST,
        preferred_element_type=jnp.float32,
    )
    stream_out = (residual.astype(jnp.float32) + moe).astype(jnp.bfloat16).reshape(stream_in.shape)
    return (stream_out, memory_state)


def solution(mesh):
    return jax.shard_map(
        body,
        mesh=mesh,
        in_specs=(
            P("grp", None, "head"),
            P("grp", None, "head"),
            P("grp", None, "head"),
            P("head"),
            P("grp", "head", None, None),
            P("head"),
            P("head", "grp"),
            P("head", None, "grp"),
            P(),
            P("head", "grp", None),
            P("head", "grp", None),
            P("head", "grp", None),
            P("head", None, None),
            P("head", None, None),
        ),
        out_specs=(P("head", None, "grp"), P("grp", "head", None, None)),
        check_vma=False,
    )
```
